256 devices in a mesh: section: 4 (over x), dp: 8 (over y, z_lo), tensor: 8 (over z_hi, core).
Axes of the slice: x: 4, y: 4, z: 8 (z_hi: 4, z_lo: 2; z = z_hi * 2 + z_lo), core: 2. Of those that a mesh axis runs over, the one named last changes fastest.
Arguments:
- activations: bfloat16 [4, 256, 4096], P('section', ('dp', 'tensor')), may hold values from -6 to 6
- w_gate: bfloat16 [4, 4096, 16384], P('section', None, ('dp', 'tensor')), may hold values from -0.09375 to 0.09375
- w_up: bfloat16 [4, 4096, 16384], P('section', None, ('dp', 'tensor')), may hold values from -0.09375 to 0.09375
- w_down: bfloat16 [4, 16384, 4096], P('section', ('dp', 'tensor')), may hold values from -0.046875 to 0.046875
- out_grad: bfloat16 [4, 256, 4096], P('section', ('dp', 'tensor')), may hold values from -6 to 6
Outputs:
- output: bfloat16 [4, 256, 4096], P('section', ('dp', 'tensor'))
- input_grad: bfloat16 [4, 256, 4096], P('section', ('dp', 'tensor'))
- grad_gate: bfloat16 [4, 4096, 16384], P('section', None, ('dp', 'tensor'))
- grad_up: bfloat16 [4, 4096, 16384], P('section', None, ('dp', 'tensor'))
- grad_down: bfloat16 [4, 16384, 4096], P('section', ('dp', 'tensor'))
The draws below stay inside these ranges and needn't reach their ends.
All inputs are finite; a program needn't handle non-finite values.
Results may differ from the reference program's by a relative error of at most 0.006.
Values may be sent and summed in bfloat16 or wider, within the bound.
No kernel may reach another device: no remote copies, remote signals or barrier semaphores. Data moves between devices by JAX's collectives and lax.ppermute only.
A program may use at most 128 MiB of HBM per device.

```python
import jax
import jax.numpy as jnp

D = 4096
FF = 16384
TOKENS = 256
SECTIONS = 4
N_SECTION = 4


def level_of(key, shape, cuts, low, high):
    def one(dim, shards_of):
        steps = jax.random.uniform(jax.random.fold_in(jax.random.fold_in(key, 6), dim), (shards_of,), jnp.float32, low / len(cuts), high / len(cuts))
        return jnp.repeat(jnp.exp(steps), shape[dim] // shards_of).reshape((-1,) + (1,) * (len(shape) - dim - 1))

    factor_of = one(*cuts[0])
    for cut in cuts[1:]:
        factor_of = factor_of * one(*cut)
    return factor_of


def noise(key, shape, deviation, most, cuts=(), held_as=jnp.bfloat16):
    factor_of = level_of(key, shape, cuts, -0.22, 0.18) if cuts else 1.0
    array = jax.random.normal(key, shape, jnp.float32) * deviation * factor_of
    return jnp.minimum(jnp.maximum(array, -most), most).astype(held_as)


def setup_inputs(seed: int = 0) -> dict:
    key_of = jax.random.split(jax.random.key(seed), 6)
    activations = noise(key_of[0], (SECTIONS, TOKENS, D), 1.0, 6.0, ((0, 4), (1, 64)))
    w_gate = noise(key_of[1], (SECTIONS, D, FF), D ** -0.5, 0.09375, ((0, 4), (2, 64)))
    w_up = noise(key_of[2], (SECTIONS, D, FF), D ** -0.5, 0.09375, ((0, 4), (2, 64)))
    w_down = noise(key_of[3], (SECTIONS, FF, D), FF ** -0.5, 0.046875, ((0, 4), (1, 64)))
    out_grad = noise(key_of[4], (SECTIONS, TOKENS, D), (16 / TOKENS ** 0.5), 6.0, ((0, 4), (1, 64)))
    return dict(activations=activations, w_gate=w_gate, w_up=w_up, w_down=w_down, out_grad=out_grad)


def swish_parts(gate):
    sigma = jax.nn.sigmoid(gate)
    return gate * sigma, sigma * (1.0 + gate * (1.0 - sigma))


def reference(activations, w_gate, w_up, w_down, out_grad):
    outputs = []
    in_grads = [None] * N_SECTION
    grads_gate = []
    grads_up = []
    grads_down = []
    for section_id in range(N_SECTION):
        source = (section_id - 1) % N_SECTION
        layer_in = activations[source]
        gate = jnp.dot(layer_in, w_gate[section_id], preferred_element_type=jnp.float32)
        upper = jnp.dot(layer_in, w_up[section_id], preferred_element_type=jnp.float32)
        swish, slope = swish_parts(gate)
        hidden = (swish * upper).astype(jnp.bfloat16)
        outputs.append(jnp.dot(hidden, w_down[section_id], preferred_element_type=jnp.float32).astype(jnp.bfloat16))
        cotangent = out_grad[section_id]
        hidden_grad = jnp.dot(cotangent, w_down[section_id].T, preferred_element_type=jnp.float32)
        grads_down.append(jnp.dot(hidden.T, cotangent, preferred_element_type=jnp.float32).astype(jnp.bfloat16))
        gate_grad = (hidden_grad * upper * slope).astype(jnp.bfloat16)
        up_grad = (hidden_grad * swish).astype(jnp.bfloat16)
        grads_gate.append(jnp.dot(layer_in.T, gate_grad, preferred_element_type=jnp.float32).astype(jnp.bfloat16))
        grads_up.append(jnp.dot(layer_in.T, up_grad, preferred_element_type=jnp.float32).astype(jnp.bfloat16))
        back = jnp.dot(gate_grad, w_gate[section_id].T, preferred_element_type=jnp.float32)
        back = back + jnp.dot(up_grad, w_up[section_id].T, preferred_element_type=jnp.float32)
        in_grads[source] = back.astype(jnp.bfloat16)
    return (jnp.stack(outputs), jnp.stack(in_grads), jnp.stack(grads_gate), jnp.stack(grads_up), jnp.stack(grads_down))
```

```python
import jax
import jax.numpy as jnp
from jax import lax
from jax.sharding import PartitionSpec as P

PLANE = ("dp", "tensor")
NY, NZ = 4, 8
BF16 = jnp.bfloat16
F32 = jnp.float32


def place(y, z, core):
    y, z = y % NY, z % NZ
    return ((y * 2 + z % 2) * 4 + z // 2) * 2 + core


CHIPS = [(y, z) for y in range(NY) for z in range(NZ)]
CORE_SWAP = [(place(y, z, c), place(y, z, 1 - c)) for y, z in CHIPS for c in (0, 1)]
Y_STEP = [(place(y, z, c), place(y + 1 - 2 * c, z, c)) for y, z in CHIPS for c in (0, 1)]
Z_STEP = [(place(y, z, c), place(y, z + 1 - 2 * c, c)) for y, z in CHIPS for c in (0, 1)]
COLOURS = [[place(k - 2 * z, z, c) for z in range(NZ)] for k in range(NY) for c in (0, 1)]


def swap(x):
    return lax.ppermute(x, PLANE, CORE_SWAP)


def y_step(x):
    return lax.ppermute(x, PLANE, Y_STEP)


def z_step(x):
    return lax.ppermute(x, PLANE, Z_STEP)


def colour_all_to_all(x):
    return lax.all_to_all(x, PLANE, 0, 0, axis_index_groups=COLOURS)


def from_behind(x, axis, by):
    length = lax.axis_size(axis)
    return lax.ppermute(x, axis, [(i, (i + by) % length) for i in range(length)])


def swish_parts(gate):
    sigma = jax.nn.sigmoid(gate)
    return (gate * sigma, sigma * (1.0 + gate * (1.0 - sigma)))


def spread(own):
    other = swap(own)
    opposite = z_step(own)
    direct = y_step(jnp.concatenate([own, other], 0))
    return jnp.concatenate([own, other, direct, swap(direct), opposite, swap(opposite)], 0)


def fold(part):
    own, other, direct, crossed, opposite, opposite_other = (
        part[:32], part[32:64], part[64:128], part[128:192], part[192:224], part[224:])
    got = swap(jnp.concatenate([other, direct, opposite_other], 0).astype(BF16)).astype(F32)
    own = own + got[:32]
    crossed = y_step((crossed + got[32:96]).astype(BF16))
    opposite = z_step((opposite + got[96:]).astype(BF16))
    return own + crossed[32:].astype(F32) + swap(crossed[:32]).astype(F32) + opposite.astype(F32)


def contract_rows(left, right):
    return lax.dot_general(left, right, (((0,), (0,)), ((), ())), preferred_element_type=F32)


def contract_cols(left, right):
    return lax.dot_general(left, right, (((1,), (1,)), ((), ())), preferred_element_type=F32)


def on_device(activations, w_gate, w_up, w_down, out_grad):
    gate_weight, up_weight, down_weight = w_gate[0], w_up[0], w_down[0]
    arrived = from_behind(activations[0], "section", 1)
    rows, width = arrived.shape
    mine = jnp.stack([arrived, out_grad[0]])
    got = colour_all_to_all(jnp.broadcast_to(mine[None], (NZ,) + mine.shape))
    layer_in = spread(got[:, 0].reshape(NZ * rows, width))
    cotangent = spread(got[:, 1].reshape(NZ * rows, width))

    gate = jnp.dot(layer_in, gate_weight, preferred_element_type=F32)
    upper = jnp.dot(layer_in, up_weight, preferred_element_type=F32)
    swish, slope = swish_parts(gate)
    hidden = (swish * upper).astype(BF16)
    out_sums = fold(jnp.dot(hidden, down_weight, preferred_element_type=F32))

    hidden_grad = contract_cols(cotangent, down_weight)
    gate_grad = (hidden_grad * upper * slope).astype(BF16)
    up_grad = (hidden_grad * swish).astype(BF16)
    back_sums = fold(contract_cols(gate_grad, gate_weight) + contract_cols(up_grad, up_weight))

    grad_down = contract_rows(hidden, cotangent).astype(BF16)
    grad_gate = contract_rows(layer_in, gate_grad).astype(BF16)
    grad_up = contract_rows(layer_in, up_grad).astype(BF16)

    sums = jnp.stack([out_sums.reshape(NZ, rows, width), back_sums.reshape(NZ, rows, width)], 1)
    final = jnp.sum(colour_all_to_all(sums.astype(BF16)).astype(F32), 0).astype(BF16)
    returned = from_behind(final[1], "section", -1)
    return (final[0][None], returned[None], grad_gate[None], grad_up[None], grad_down[None])


def solution(mesh):
    return jax.shard_map(
        on_device,
        mesh=mesh,
        in_specs=(
            P("section", PLANE, None),
            P("section", None, PLANE),
            P("section", None, PLANE),
            P("section", PLANE, None),
            P("section", PLANE, None),
        ),
        out_specs=(
            P("section", PLANE, None),
            P("section", PLANE, None),
            P("section", None, PLANE),
            P("section", None, PLANE),
            P("section", PLANE, None),
        ),
        check_vma=False,
    )
```

```python
import jax
import jax.numpy as jnp
from jax import lax
from jax.experimental import pallas as pl
from jax.experimental.pallas import tpu as pltpu
from jax.sharding import PartitionSpec as P

PLANE = ("dp", "tensor")
NY, NZ = 4, 8
BF16 = jnp.bfloat16
F32 = jnp.float32
CHUNK = 1024


def place(y, z, core):
    y, z = y % NY, z % NZ
    return ((y * 2 + z % 2) * 4 + z // 2) * 2 + core


CHIPS = [(y, z) for y in range(NY) for z in range(NZ)]
CORE_SWAP = [(place(y, z, c), place(y, z, 1 - c)) for y, z in CHIPS for c in (0, 1)]
Y_NEXT = [(place(y, z, c), place(y + 1, z, c)) for y, z in CHIPS for c in (0, 1)]
Y_LAST = [(place(y, z, c), place(y - 1, z, c)) for y, z in CHIPS for c in (0, 1)]
Z_STEP = [(place(y, z, c), place(y, z + 1 - 2 * c, c)) for y, z in CHIPS for c in (0, 1)]
COLOURS = [[place(k - 2 * z, z, c) for z in range(NZ)] for k in range(NY) for c in (0, 1)]


def swap(x):
    return lax.ppermute(x, PLANE, CORE_SWAP)


def y_next(x):
    return lax.ppermute(x, PLANE, Y_NEXT)


def y_last(x):
    return lax.ppermute(x, PLANE, Y_LAST)


def z_step(x):
    return lax.ppermute(x, PLANE, Z_STEP)


def colour_all_to_all(x):
    return lax.all_to_all(x, PLANE, 0, 0, axis_index_groups=COLOURS)


def from_behind(x, axis, by):
    length = lax.axis_size(axis)
    return lax.ppermute(x, axis, [(i, (i + by) % length) for i in range(length)])


def contract_rows(left, right):
    return lax.dot_general(left, right, (((0,), (0,)), ((), ())), preferred_element_type=F32)


def contract_cols(left, right):
    return lax.dot_general(left, right, (((1,), (1,)), ((), ())), preferred_element_type=F32)


def local_kernel(body, shapes, *args):
    return pl.pallas_call(
        body,
        out_shape=[jax.ShapeDtypeStruct(shape, dtype) for shape, dtype in shapes],
        in_specs=[pl.BlockSpec(memory_space=pltpu.VMEM)] * len(args),
        out_specs=[pl.BlockSpec(memory_space=pltpu.VMEM)] * len(shapes),
        compiler_params=pltpu.CompilerParams(vmem_limit_bytes=32 * 2**20),
        cost_estimate=pl.CostEstimate(flops=0, bytes_accessed=0, transcendentals=0),
    )(*args)


def load_body(*refs):
    half = (len(refs) - 1) // 2
    done = refs[-1]
    copies = [pltpu.make_async_copy(refs[i], refs[half + i], done.at[i]) for i in range(half)]
    for copy in copies:
        copy.start()
    for copy in copies:
        copy.wait()


def load(*args):
    return pl.pallas_call(
        load_body,
        out_shape=[jax.ShapeDtypeStruct(a.shape, a.dtype) for a in args],
        in_specs=[pl.BlockSpec(memory_space=pl.ANY)] * len(args),
        out_specs=[pl.BlockSpec(memory_space=pl.ANY)] * len(args),
        scratch_shapes=[pltpu.SemaphoreType.DMA((len(args),))],
        compiler_params=pltpu.CompilerParams(vmem_limit_bytes=16 * 2**20),
        cost_estimate=pl.CostEstimate(flops=0, bytes_accessed=0, transcendentals=0),
    )(*args)


def after(x, *earlier):
    return lax.optimization_barrier((x, *earlier))[0]


def split_body(got_ref, own_ref):
    for kind in (0, 1):
        for pair in range(NZ // 2):
            two = [got_ref[2 * pair + i, kind].astype(F32) for i in (0, 1)]
            own_ref[kind, 8 * pair : 8 * pair + 8, :] = jnp.concatenate(two, 0).astype(BF16)


def forward_body(*refs):
    blocks, (gate_w, up_w, down_w), (layer, hidden, swish, rise, other) = refs[:8], refs[8:11], refs[11:]
    for i, block in enumerate(blocks):
        layer[32 * i : 32 * i + 32, :] = block[0]
    gate = jnp.dot(layer[...], gate_w[0], preferred_element_type=F32)
    upper = jnp.dot(layer[...], up_w[0], preferred_element_type=F32)
    sigma = jax.nn.sigmoid(gate)
    swish[...] = gate * sigma
    rise[...] = upper * (sigma * (1.0 + gate * (1.0 - sigma)))
    hidden[...] = (swish[...] * upper).astype(BF16)

    @pl.loop(0, down_w.shape[2], step=CHUNK)
    def _(start):
        columns = pl.ds(pl.multiple_of(start, CHUNK), CHUNK)
        other[:, columns] = jnp.dot(hidden[128:, :], down_w[0, :, columns], preferred_element_type=F32).astype(BF16)


def backward_body(*refs):
    blocks, (down_w, swish, rise), (cotangent, gate_grad, up_grad) = refs[:8], refs[8:11], refs[11:]
    for i, block in enumerate(blocks):
        cotangent[32 * i : 32 * i + 32, :] = block[1]
    hidden_grad = contract_cols(cotangent[...], down_w[0])
    gate_grad[...] = (hidden_grad * rise[...]).astype(BF16)
    up_grad[...] = (hidden_grad * swish[...]).astype(BF16)


def back_other_body(gate_grad, up_grad, gate_w, up_w, other):
    @pl.loop(0, gate_w.shape[1], step=CHUNK)
    def _(start):
        columns = pl.ds(pl.multiple_of(start, CHUNK), CHUNK)
        back = contract_cols(gate_grad[128:, :], gate_w[0, columns, :])
        back += contract_cols(up_grad[128:, :], up_w[0, columns, :])
        other[:, columns] = back.astype(BF16)


def put_sums(sums, columns, own, last, next_, step):
    own[:, columns] = sums[:32]
    last[:, columns] = sums[32:64].astype(BF16)
    next_[:, columns] = sums[64:96].astype(BF16)
    step[:, columns] = sums[96:].astype(BF16)


def out_sums_body(hidden, down_w, got, own, last, next_, step):
    @pl.loop(0, down_w.shape[2], step=CHUNK)
    def _(start):
        columns = pl.ds(pl.multiple_of(start, CHUNK), CHUNK)
        sums = jnp.dot(hidden[:128, :], down_w[0, :, columns], preferred_element_type=F32)
        put_sums(sums + got[:, columns].astype(F32), columns, own, last, next_, step)


def back_sums_body(gate_grad, up_grad, gate_w, up_w, got, own, last, next_, step):
    @pl.loop(0, gate_w.shape[1], step=CHUNK)
    def _(start):
        columns = pl.ds(pl.multiple_of(start, CHUNK), CHUNK)
        sums = contract_cols(gate_grad[:128, :], gate_w[0, columns, :])
        sums += contract_cols(up_grad[:128, :], up_w[0, columns, :])
        put_sums(sums + got[:, columns].astype(F32), columns, own, last, next_, step)


def join_body(*refs):
    joined = refs[8]
    for kind in (0, 1):
        own, *received = refs[4 * kind : 4 * kind + 4]
        for pair in range(NZ // 2):
            rows = slice(8 * pair, 8 * pair + 8)
            sums = own[rows, :]
            for term in received:
                sums = sums + term[rows, :].astype(F32)
            for i in (0, 1):
                joined[2 * pair + i, kind] = sums[4 * i : 4 * i + 4].astype(BF16)


def send_sums(own, last, next_, step):
    return [own, y_last(last), y_next(next_), z_step(step)]


def on_device(activations, w_gate, w_up, w_down, out_grad):
    arrived = from_behind(activations[0], "section", 1)
    mine = jnp.stack([arrived, out_grad[0]])
    _, rows, width = mine.shape
    units = w_down.shape[1]
    tokens = 2 * NY * NZ * rows
    got = colour_all_to_all(jnp.broadcast_to(mine[None], (NZ,) + mine.shape))

    (own,) = local_kernel(split_body, [((2, NZ * rows, width), BF16)], got)
    step, last, next_ = z_step(own), y_last(own), y_next(own)
    w_gate, w_up, w_down = load(after(w_gate, step), w_up, w_down)
    next_, last = lax.optimization_barrier((next_, last, w_gate))[:2]
    blocks = [own, next_, last, step]
    blocks = blocks + [swap(block) for block in blocks]

    send = ((NZ * rows, width), BF16)
    sends = [((NZ * rows, width), F32), send, send, send]
    layer_in, hidden, swish, rise, out_other = local_kernel(
        forward_body,
        [((tokens, width), BF16), ((tokens, units), BF16), ((tokens, units), F32), ((tokens, units), F32),
         ((tokens // 2, width), BF16)],
        *blocks, w_gate, w_up, w_down)
    out_got = swap(out_other)
    cotangent, gate_grad, up_grad = local_kernel(
        backward_body,
        [((tokens, width), BF16), ((tokens, units), BF16), ((tokens, units), BF16)],
        *blocks, w_down, swish, rise)
    (back_other,) = local_kernel(
        back_other_body, [((tokens // 2, width), BF16)], after(gate_grad, out_got), up_grad, w_gate, w_up)
    out_sums = local_kernel(out_sums_body, sends, hidden, w_down, out_got)
    back_got = after(swap(back_other), out_sums[0])
    out_terms = send_sums(*out_sums)
    back_terms = send_sums(*local_kernel(back_sums_body, sends, gate_grad, up_grad, w_gate, w_up, back_got))

    grad_down = contract_rows(hidden, cotangent).astype(BF16)
    grad_gate = contract_rows(layer_in, gate_grad).astype(BF16)
    grad_up = contract_rows(layer_in, up_grad).astype(BF16)

    (sums,) = local_kernel(join_body, [((NZ, 2, rows, width), BF16)], *out_terms, *back_terms)
    arrived = colour_all_to_all(sums)
    arrived, grad_gate, grad_up, grad_down = lax.optimization_barrier((arrived, grad_gate, grad_up, grad_down))
    final = jnp.sum(arrived.astype(F32), 0).astype(BF16)
    returned = from_behind(final[1], "section", -1)
    return (final[0][None], returned[None], grad_gate[None], grad_up[None], grad_down[None])


def solution(mesh):
    return jax.shard_map(
        on_device,
        mesh=mesh,
        in_specs=(
            P("section", PLANE, None),
            P("section", None, PLANE),
            P("section", None, PLANE),
            P("section", PLANE, None),
            P("section", PLANE, None),
        ),
        out_specs=(
            P("section", PLANE, None),
            P("section", PLANE, None),
            P("section", None, PLANE),
            P("section", None, PLANE),
            P("section", PLANE, None),
        ),
        check_vma=False,
    )
```

```python
import jax
import jax.numpy as jnp
from jax import lax
from jax.experimental import pallas as pl
from jax.experimental.pallas import tpu as pltpu
from jax.sharding import PartitionSpec as P

PLANE = ("dp", "tensor")
NY, NZ = 4, 8
BF16 = jnp.bfloat16
F32 = jnp.float32
CHUNK = 1024


def place(y, z, core):
    y, z = y % NY, z % NZ
    return ((y * 2 + z % 2) * 4 + z // 2) * 2 + core


CHIPS = [(y, z) for y in range(NY) for z in range(NZ)]
CORE_SWAP = [(place(y, z, c), place(y, z, 1 - c)) for y, z in CHIPS for c in (0, 1)]
Y_NEXT = [(place(y, z, c), place(y + 1, z, c)) for y, z in CHIPS for c in (0, 1)]
Y_LAST = [(place(y, z, c), place(y - 1, z, c)) for y, z in CHIPS for c in (0, 1)]
Z_STEP = [(place(y, z, c), place(y, z + 1 - 2 * c, c)) for y, z in CHIPS for c in (0, 1)]
COLOURS = [[place(k - 2 * z, z, c) for z in range(NZ)] for k in range(NY) for c in (0, 1)]


def swap(x):
    return lax.ppermute(x, PLANE, CORE_SWAP)


def y_next(x):
    return lax.ppermute(x, PLANE, Y_NEXT)


def y_last(x):
    return lax.ppermute(x, PLANE, Y_LAST)


def z_step(x):
    return lax.ppermute(x, PLANE, Z_STEP)


def colour_all_to_all(x):
    return lax.all_to_all(x, PLANE, 0, 0, axis_index_groups=COLOURS)


def from_behind(x, axis, by):
    length = lax.axis_size(axis)
    return lax.ppermute(x, axis, [(i, (i + by) % length) for i in range(length)])


def contract_rows(left, right):
    return lax.dot_general(left, right, (((0,), (0,)), ((), ())), preferred_element_type=F32)


def contract_cols(left, right):
    return lax.dot_general(left, right, (((1,), (1,)), ((), ())), preferred_element_type=F32)


def local_kernel(body, shapes, *args, scratch=()):
    return pl.pallas_call(
        body,
        out_shape=[jax.ShapeDtypeStruct(shape, dtype) for shape, dtype in shapes],
        in_specs=[pl.BlockSpec(memory_space=pltpu.VMEM)] * len(args),
        out_specs=[pl.BlockSpec(memory_space=pltpu.VMEM)] * len(shapes),
        scratch_shapes=list(scratch),
        compiler_params=pltpu.CompilerParams(vmem_limit_bytes=32 * 2**20),
        cost_estimate=pl.CostEstimate(flops=0, bytes_accessed=0, transcendentals=0),
    )(*args)


def load_body(*refs):
    half = (len(refs) - 1) // 2
    done = refs[-1]
    copies = [pltpu.make_async_copy(refs[i], refs[half + i], done.at[i]) for i in range(half)]
    for copy in copies:
        copy.start()
    for copy in copies:
        copy.wait()


def load(*args):
    return pl.pallas_call(
        load_body,
        out_shape=[jax.ShapeDtypeStruct(a.shape, a.dtype) for a in args],
        in_specs=[pl.BlockSpec(memory_space=pl.ANY)] * len(args),
        out_specs=[pl.BlockSpec(memory_space=pl.ANY)] * len(args),
        scratch_shapes=[pltpu.SemaphoreType.DMA((len(args),))],
        compiler_params=pltpu.CompilerParams(vmem_limit_bytes=16 * 2**20),
        cost_estimate=pl.CostEstimate(flops=0, bytes_accessed=0, transcendentals=0),
    )(*args)


def after(x, *earlier):
    return lax.optimization_barrier((x, *earlier))[0]


def split_body(got_ref, own_ref):
    for kind in (0, 1):
        for pair in range(NZ // 2):
            two = [got_ref[2 * pair + i, kind].astype(F32) for i in (0, 1)]
            own_ref[kind, 8 * pair : 8 * pair + 8, :] = jnp.concatenate(two, 0).astype(BF16)


def put_sums(sums, columns, own, last, next_, step):
    own[:, columns] = sums[:32]
    last[:, columns] = sums[32:64].astype(BF16)
    next_[:, columns] = sums[64:96].astype(BF16)
    step[:, columns] = sums[96:].astype(BF16)


def forward_body(*refs):
    blocks, gate_ws, up_ws, down_ws = refs[:4], refs[4:6], refs[6:8], refs[8:10]
    hiddens, swish, rise, sends, layer = refs[10:12], refs[12], refs[13], refs[14:18], refs[18]
    for i, block in enumerate(blocks):
        layer[32 * i : 32 * i + 32, :] = block[0]
    for core in (0, 1):
        gate = jnp.dot(layer[...], gate_ws[core][0], preferred_element_type=F32)
        upper = jnp.dot(layer[...], up_ws[core][0], preferred_element_type=F32)
        sigma = jax.nn.sigmoid(gate)
        swish[core] = gate * sigma
        rise[core] = upper * (sigma * (1.0 + gate * (1.0 - sigma)))
        hiddens[core][...] = (swish[core] * upper).astype(BF16)

    @pl.loop(0, down_ws[0].shape[2], step=CHUNK)
    def _(start):
        columns = pl.ds(pl.multiple_of(start, CHUNK), CHUNK)
        sums = sum(
            jnp.dot(hiddens[core][...], down_ws[core][0, :, columns], preferred_element_type=F32) for core in (0, 1)
        )
        put_sums(sums, columns, *sends)


def backward_body(*refs):
    blocks, gate_ws, up_ws, down_ws, (swish, rise, hidden) = refs[:4], refs[4:6], refs[6:8], refs[8:10], refs[10:13]
    gate_grads, up_grads, sends, cotangent = (refs[13], refs[15].at[0]), (refs[14], refs[15].at[1]), refs[16:20], refs[20]
    refs[15][2] = hidden[...]
    for i, block in enumerate(blocks):
        cotangent[32 * i : 32 * i + 32, :] = block[1]
    for core in (0, 1):
        hidden_grad = contract_cols(cotangent[...], down_ws[core][0])
        gate_grads[core][...] = (hidden_grad * rise[core]).astype(BF16)
        up_grads[core][...] = (hidden_grad * swish[core]).astype(BF16)

    @pl.loop(0, gate_ws[0].shape[1], step=CHUNK)
    def _(start):
        columns = pl.ds(pl.multiple_of(start, CHUNK), CHUNK)
        sums = sum(
            contract_cols(gate_grads[core][...], gate_ws[core][0, columns, :])
            + contract_cols(up_grads[core][...], up_ws[core][0, columns, :])
            for core in (0, 1)
        )
        put_sums(sums, columns, *sends)


def weight_grads_body(*refs):
    blocks = refs[:8]
    gate_grad, up_grad, hidden = [(refs[8 + i], refs[11].at[i]) for i in range(3)]
    into_gate, into_up, into_down = refs[12:]
    layer = jnp.concatenate([block[0] for block in blocks], 0)
    for grad, into in ((gate_grad, into_gate), (up_grad, into_up)):
        grad = jnp.concatenate([grad[0][...], grad[1][...]], 0)
        into[0] = contract_rows(layer, grad).astype(BF16)
    hidden = jnp.concatenate([hidden[0][...], hidden[1][...]], 0)
    cotangent = jnp.concatenate([block[1] for block in blocks], 0)
    into_down[0] = contract_rows(hidden, cotangent).astype(BF16)


def weight_grads(*args):
    _, rows, width = args[0].shape
    tokens, units = args[8].shape
    part = width // 8
    streamed = [pl.BlockSpec((2, rows, part), lambda i: (0, 0, i))] * 8
    whole = [pl.BlockSpec((tokens, units), lambda i: (0, 0))] * 3 + [pl.BlockSpec((3, tokens, units), lambda i: (0, 0, 0))]
    across = [pl.BlockSpec((1, part, units), lambda i: (0, i, 0))] * 2
    along = [pl.BlockSpec((1, units, part), lambda i: (0, 0, i))]
    shapes = [(1, width, units), (1, width, units), (1, units, width)]
    return pl.pallas_call(
        weight_grads_body,
        grid=(width // part,),
        out_shape=[jax.ShapeDtypeStruct(shape, BF16) for shape in shapes],
        in_specs=streamed + whole,
        out_specs=across + along,
        compiler_params=pltpu.CompilerParams(vmem_limit_bytes=32 * 2**20),
        cost_estimate=pl.CostEstimate(flops=0, bytes_accessed=0, transcendentals=0),
    )(*args)


def join_body(*refs):
    joined = refs[8]
    for kind in (0, 1):
        own, *received = refs[4 * kind : 4 * kind + 4]
        for pair in range(NZ // 2):
            rows = slice(8 * pair, 8 * pair + 8)
            sums = own[rows, :]
            for term in received:
                sums = sums + term[rows, :].astype(F32)
            for i in (0, 1):
                joined[2 * pair + i, kind] = sums[4 * i : 4 * i + 4].astype(BF16)


def send_sums(own, last, next_, step):
    return [own, y_last(last), y_next(next_), z_step(step)]


def on_device(activations, w_gate, w_up, w_down, out_grad):
    arrived = from_behind(activations[0], "section", 1)
    mine = jnp.stack([arrived, out_grad[0]])
    _, rows, width = mine.shape
    units = w_down.shape[1]
    tokens = NY * NZ * rows
    got = colour_all_to_all(jnp.broadcast_to(mine[None], (NZ,) + mine.shape))

    got, *partner = lax.optimization_barrier((got, swap(w_gate), swap(w_up), swap(w_down)))

    (own,) = local_kernel(split_body, [((2, NZ * rows, width), BF16)], got)
    step, last, next_ = z_step(own), y_last(own), y_next(own)
    loaded = load(after(w_gate, step), w_up, w_down)
    blocks = [own, after(next_, loaded[0]), last, step]
    weights = [w for pair in zip(loaded, partner) for w in pair]

    send = ((NZ * rows, width), BF16)
    sends = [((NZ * rows, width), F32), send, send, send]
    some = ((tokens, units), BF16)
    scratch = [pltpu.VMEM((tokens, width), BF16)]
    kept = ((2, tokens, units), F32)
    hidden, hidden_other, swish, rise, *out_sums = local_kernel(
        forward_body, [some, some, kept, kept, *sends], *blocks, *weights, scratch=scratch)
    out_terms = send_sums(*out_sums)
    gate_grad, up_grad, give, *back_sums = local_kernel(
        backward_body, [some, some, ((3, tokens, units), BF16), *sends],
        *blocks, *weights, swish, rise, hidden_other, scratch=scratch)
    back_terms = send_sums(*back_sums)

    (sums,) = local_kernel(join_body, [((NZ, 2, rows, width), BF16)], *out_terms, *back_terms)

    *blocks, give = lax.optimization_barrier((*blocks, give, sums))[:-1]
    grad_gate, grad_up, grad_down = weight_grads(
        *blocks, *[swap(block) for block in blocks], gate_grad, up_grad, hidden, swap(give))
    arrived = colour_all_to_all(sums)
    arrived, grad_gate, grad_up, grad_down = lax.optimization_barrier((arrived, grad_gate, grad_up, grad_down))
    final = jnp.sum(arrived.astype(F32), 0).astype(BF16)
    returned = from_behind(final[1], "section", -1)
    return (final[0][None], returned[None], grad_gate, grad_up, grad_down)


def solution(mesh):
    return jax.shard_map(
        on_device,
        mesh=mesh,
        in_specs=(
            P("section", PLANE, None),
            P("section", None, PLANE),
            P("section", None, PLANE),
            P("section", PLANE, None),
            P("section", PLANE, None),
        ),
        out_specs=(
            P("section", PLANE, None),
            P("section", PLANE, None),
            P("section", None, PLANE),
            P("section", None, PLANE),
            P("section", PLANE, None),
        ),
        check_vma=False,
    )
```

```python
import jax
import jax.numpy as jnp
from jax import lax
from jax.experimental import pallas as pl
from jax.experimental.pallas import tpu as pltpu
from jax.sharding import PartitionSpec as P

PLANE = ("dp", "tensor")
NY, NZ = 4, 8
BF16 = jnp.bfloat16
F32 = jnp.float32
CHUNK = 1024


def place(y, z, core):
    y, z = y % NY, z % NZ
    return ((y * 2 + z % 2) * 4 + z // 2) * 2 + core


CHIPS = [(y, z) for y in range(NY) for z in range(NZ)]
CORE_SWAP = [(place(y, z, c), place(y, z, 1 - c)) for y, z in CHIPS for c in (0, 1)]
Y_NEXT = [(place(y, z, c), place(y + 1, z, c)) for y, z in CHIPS for c in (0, 1)]
Y_LAST = [(place(y, z, c), place(y - 1, z, c)) for y, z in CHIPS for c in (0, 1)]
Z_STEP = [(place(y, z, c), place(y, z + 1 - 2 * c, c)) for y, z in CHIPS for c in (0, 1)]
COLOURS = [[place(k - 2 * z, z, c) for z in range(NZ)] for k in range(NY) for c in (0, 1)]


def swap(x):
    return lax.ppermute(x, PLANE, CORE_SWAP)


def y_next(x):
    return lax.ppermute(x, PLANE, Y_NEXT)


def y_last(x):
    return lax.ppermute(x, PLANE, Y_LAST)


def z_step(x):
    return lax.ppermute(x, PLANE, Z_STEP)


def colour_all_to_all(x):
    return lax.all_to_all(x, PLANE, 0, 0, axis_index_groups=COLOURS)


def from_behind(x, axis, by):
    length = lax.axis_size(axis)
    return lax.ppermute(x, axis, [(i, (i + by) % length) for i in range(length)])


def contract_rows(left, right):
    return lax.dot_general(left, right, (((0,), (0,)), ((), ())), preferred_element_type=F32)


def contract_cols(left, right):
    return lax.dot_general(left, right, (((1,), (1,)), ((), ())), preferred_element_type=F32)


def local_kernel(body, shapes, *args, scratch=()):
    return pl.pallas_call(
        body,
        out_shape=[jax.ShapeDtypeStruct(shape, dtype) for shape, dtype in shapes],
        in_specs=[pl.BlockSpec(memory_space=pltpu.VMEM)] * len(args),
        out_specs=[pl.BlockSpec(memory_space=pltpu.VMEM)] * len(shapes),
        scratch_shapes=list(scratch),
        compiler_params=pltpu.CompilerParams(vmem_limit_bytes=24 * 2**20),
        cost_estimate=pl.CostEstimate(flops=0, bytes_accessed=0, transcendentals=0),
    )(*args)


def load_body(*refs):
    half = (len(refs) - 1) // 2
    done = refs[-1]
    copies = [pltpu.make_async_copy(refs[i], refs[half + i], done.at[i]) for i in range(half)]
    for copy in copies:
        copy.start()
    for copy in copies:
        copy.wait()


def load(*args):
    return pl.pallas_call(
        load_body,
        out_shape=[jax.ShapeDtypeStruct(a.shape, a.dtype) for a in args],
        in_specs=[pl.BlockSpec(memory_space=pl.ANY)] * len(args),
        out_specs=[pl.BlockSpec(memory_space=pl.ANY)] * len(args),
        scratch_shapes=[pltpu.SemaphoreType.DMA((len(args),))],
        compiler_params=pltpu.CompilerParams(vmem_limit_bytes=16 * 2**20),
        cost_estimate=pl.CostEstimate(flops=0, bytes_accessed=0, transcendentals=0),
    )(*args)


def after(x, *earlier):
    return lax.optimization_barrier((x, *earlier))[0]


def fan_body(layer, cotangent, fan):
    for i in range(NZ):
        fan[i, 0] = layer[...]
        fan[i, 1] = cotangent[0]


def total_body(arrived, output, back):
    for kind, total in enumerate((output, back)):
        total[0] = sum(arrived[i, kind].astype(F32) for i in range(NZ)).astype(BF16)


def split_body(got_ref, own_ref):
    for kind in (0, 1):
        for pair in range(NZ // 2):
            two = [got_ref[2 * pair + i, kind].astype(F32) for i in (0, 1)]
            own_ref[kind, 8 * pair : 8 * pair + 8, :] = jnp.concatenate(two, 0).astype(BF16)


def put_sums(sums, columns, own, last, next_, step):
    own[:, columns] = sums[:32]
    last[:, columns] = sums[32:64].astype(BF16)
    next_[:, columns] = sums[64:96].astype(BF16)
    step[:, columns] = sums[96:].astype(BF16)


def forward_body(*refs):
    blocks, gate_ws, up_ws, down_ws = refs[:4], refs[4:6], refs[6:8], refs[8:10]
    hiddens, swish, rise, sends, layer = refs[10:12], refs[12], refs[13], refs[14:18], refs[18]
    for i, block in enumerate(blocks):
        layer[32 * i : 32 * i + 32, :] = block[0]
    for core in (0, 1):
        gate = jnp.dot(layer[...], gate_ws[core][0], preferred_element_type=F32)
        upper = jnp.dot(layer[...], up_ws[core][0], preferred_element_type=F32)
        sigma = jax.nn.sigmoid(gate)
        swish[core] = gate * sigma
        rise[core] = upper * (sigma * (1.0 + gate * (1.0 - sigma)))
        hiddens[core][...] = (swish[core] * upper).astype(BF16)

    @pl.loop(0, down_ws[0].shape[2], step=CHUNK)
    def _(start):
        columns = pl.ds(pl.multiple_of(start, CHUNK), CHUNK)
        sums = sum(
            jnp.dot(hiddens[core][...], down_ws[core][0, :, columns], preferred_element_type=F32) for core in (0, 1)
        )
        put_sums(sums, columns, *sends)


def turn_body(gate_w, up_w, gate_x, up_x, down_w, down_x, across, down):
    units = gate_w.shape[2]
    for i, source in enumerate((gate_w, up_w, gate_x, up_x)):

        @pl.loop(0, source.shape[1], step=CHUNK)
        def _(start):
            columns = pl.ds(pl.multiple_of(start, CHUNK), CHUNK)
            across[i * units : (i + 1) * units, columns] = source[0, columns, :].T

    for i, source in enumerate((down_w, down_x)):

        @pl.loop(0, source.shape[2], step=CHUNK)
        def _(start):
            columns = pl.ds(pl.multiple_of(start, CHUNK), CHUNK)
            down[columns, i * units : (i + 1) * units] = source[0, :, columns].T


def backward_body(*refs):
    blocks, across, down, (swish, rise, hidden) = refs[:4], refs[4], refs[5], refs[6:9]
    gate_grad, up_grad, give, sends, cotangent, grads = refs[9], refs[10], refs[11], refs[12:16], refs[16], refs[17]
    units = hidden.shape[1]
    give[2] = hidden[...]
    for i, block in enumerate(blocks):
        cotangent[32 * i : 32 * i + 32, :] = block[1]
    hidden_grads = jnp.dot(cotangent[...], down[...], preferred_element_type=F32)
    for core, (to_gate, to_up) in enumerate(((gate_grad, up_grad), (give.at[0], give.at[1]))):
        hidden_grad = hidden_grads[:, core * units : (core + 1) * units]
        to_gate[...] = (hidden_grad * rise[core]).astype(BF16)
        to_up[...] = (hidden_grad * swish[core]).astype(BF16)
        grads[:, 2 * core * units : (2 * core + 1) * units] = to_gate[...]
        grads[:, (2 * core + 1) * units : 2 * (core + 1) * units] = to_up[...]

    @pl.loop(0, across.shape[1], step=CHUNK)
    def _(start):
        columns = pl.ds(pl.multiple_of(start, CHUNK), CHUNK)
        put_sums(jnp.dot(grads[...], across[:, columns], preferred_element_type=F32), columns, *sends)


def weight_grads_body(*refs):
    blocks = refs[:8]
    gate_grad, up_grad, hidden = [(refs[8 + i], refs[11].at[i]) for i in range(3)]
    into_gate, into_up, into_down = refs[12:]
    layer = jnp.concatenate([block[0] for block in blocks], 0)
    for grad, into in ((gate_grad, into_gate), (up_grad, into_up)):
        grad = jnp.concatenate([grad[0][...], grad[1][...]], 0)
        into[0] = contract_rows(layer, grad).astype(BF16)
    hidden = jnp.concatenate([hidden[0][...], hidden[1][...]], 0)
    cotangent = jnp.concatenate([block[1] for block in blocks], 0)
    into_down[0] = contract_rows(hidden, cotangent).astype(BF16)


def weight_grads(*args):
    _, rows, width = args[0].shape
    tokens, units = args[8].shape
    part = width // 8
    streamed = [pl.BlockSpec((2, rows, part), lambda i: (0, 0, i))] * 8
    whole = [pl.BlockSpec((tokens, units), lambda i: (0, 0))] * 3 + [pl.BlockSpec((3, tokens, units), lambda i: (0, 0, 0))]
    across = [pl.BlockSpec((1, part, units), lambda i: (0, i, 0))] * 2
    along = [pl.BlockSpec((1, units, part), lambda i: (0, 0, i))]
    shapes = [(1, width, units), (1, width, units), (1, units, width)]
    return pl.pallas_call(
        weight_grads_body,
        grid=(width // part,),
        out_shape=[jax.ShapeDtypeStruct(shape, BF16) for shape in shapes],
        in_specs=streamed + whole,
        out_specs=across + along,
        compiler_params=pltpu.CompilerParams(vmem_limit_bytes=24 * 2**20),
        cost_estimate=pl.CostEstimate(flops=0, bytes_accessed=0, transcendentals=0),
    )(*args)


def join_body(*refs):
    joined = refs[8]
    for kind in (0, 1):
        own, *received = refs[4 * kind : 4 * kind + 4]
        for pair in range(NZ // 2):
            rows = slice(8 * pair, 8 * pair + 8)
            sums = own[rows, :]
            for term in received:
                sums = sums + term[rows, :].astype(F32)
            for i in (0, 1):
                joined[2 * pair + i, kind] = sums[4 * i : 4 * i + 4].astype(BF16)


def send_sums(own, last, next_, step):
    return [own, y_last(last), y_next(next_), z_step(step)]


def on_device(activations, w_gate, w_up, w_down, out_grad):
    arrived = from_behind(activations[0], "section", 1)
    rows, width = arrived.shape
    units = w_down.shape[1]
    tokens = NY * NZ * rows
    (mine,) = local_kernel(fan_body, [((NZ, 2, rows, width), BF16)], arrived, out_grad)
    got = colour_all_to_all(mine)

    got, *partner = lax.optimization_barrier((got, swap(w_gate), swap(w_up), swap(w_down)))

    (own,) = local_kernel(split_body, [((2, NZ * rows, width), BF16)], got)
    step, last, next_ = z_step(own), y_last(own), y_next(own)
    loaded = load(after(w_gate, own), w_up, w_down)
    weights = [w for pair in zip(loaded, partner) for w in pair]
    turned = local_kernel(
        turn_body, [((4 * units, width), BF16), ((width, 2 * units), BF16)],
        loaded[0], loaded[1], partner[0], partner[1], loaded[2], partner[2])
    blocks = [own, after(next_, *turned), last, step]

    send = ((NZ * rows, width), BF16)
    sends = [((NZ * rows, width), F32), send, send, send]
    some = ((tokens, units), BF16)
    scratch = [pltpu.VMEM((tokens, width), BF16)]
    kept = ((2, tokens, units), F32)
    hidden, hidden_other, swish, rise, *out_sums = local_kernel(
        forward_body, [some, some, kept, kept, *sends], *blocks, *weights, scratch=scratch)
    out_terms = send_sums(*out_sums)
    gate_grad, up_grad, give, *back_sums = local_kernel(
        backward_body, [some, some, ((3, tokens, units), BF16), *sends],
        *blocks, *turned, swish, rise, hidden_other,
        scratch=scratch + [pltpu.VMEM((tokens, 4 * units), BF16)])
    back_terms = send_sums(*back_sums)

    (sums,) = local_kernel(join_body, [((NZ, 2, rows, width), BF16)], *out_terms, *back_terms)

    *blocks, give = lax.optimization_barrier((*blocks, give, sums))[:-1]
    grad_gate, grad_up, grad_down = weight_grads(
        *blocks, *[swap(block) for block in blocks], gate_grad, up_grad, hidden, swap(give))
    arrived = colour_all_to_all(sums)
    arrived, grad_gate, grad_up, grad_down = lax.optimization_barrier((arrived, grad_gate, grad_up, grad_down))
    output, back = local_kernel(total_body, [((1, rows, width), BF16)] * 2, arrived)
    return (output, from_behind(back, "section", -1), grad_gate, grad_up, grad_down)


def solution(mesh):
    return jax.shard_map(
        on_device,
        mesh=mesh,
        in_specs=(
            P("section", PLANE, None),
            P("section", None, PLANE),
            P("section", None, PLANE),
            P("section", PLANE, None),
            P("section", PLANE, None),
        ),
        out_specs=(
            P("section", PLANE, None),
            P("section", PLANE, None),
            P("section", None, PLANE),
            P("section", None, PLANE),
            P("section", PLANE, None),
        ),
        check_vma=False,
    )
```

```python
import jax
import jax.numpy as jnp
from jax import lax
from jax.experimental import pallas as pl
from jax.experimental.pallas import tpu as pltpu
from jax.sharding import PartitionSpec as P

PLANE = ("dp", "tensor")
NY, NZ = 4, 8
BF16 = jnp.bfloat16
F32 = jnp.float32
CHUNK = 1024


def place(y, z, core):
    y, z = y % NY, z % NZ
    return ((y * 2 + z % 2) * 4 + z // 2) * 2 + core


CHIPS = [(y, z) for y in range(NY) for z in range(NZ)]
CORE_SWAP = [(place(y, z, c), place(y, z, 1 - c)) for y, z in CHIPS for c in (0, 1)]
Y_NEXT = [(place(y, z, c), place(y + 1, z, c)) for y, z in CHIPS for c in (0, 1)]
Y_LAST = [(place(y, z, c), place(y - 1, z, c)) for y, z in CHIPS for c in (0, 1)]
Z_STEP = [(place(y, z, c), place(y, z + 1 - 2 * c, c)) for y, z in CHIPS for c in (0, 1)]
COLOURS = [[place(k - 2 * z, z, c) for z in range(NZ)] for k in range(NY) for c in (0, 1)]


def swap(x):
    return lax.ppermute(x, PLANE, CORE_SWAP)


def y_next(x):
    return lax.ppermute(x, PLANE, Y_NEXT)


def y_last(x):
    return lax.ppermute(x, PLANE, Y_LAST)


def z_step(x):
    return lax.ppermute(x, PLANE, Z_STEP)


def colour_all_to_all(x):
    return lax.all_to_all(x, PLANE, 0, 0, axis_index_groups=COLOURS)


def from_behind(x, axis, by):
    length = lax.axis_size(axis)
    return lax.ppermute(x, axis, [(i, (i + by) % length) for i in range(length)])


def contract_rows(left, right):
    return lax.dot_general(left, right, (((0,), (0,)), ((), ())), preferred_element_type=F32)


def contract_cols(left, right):
    return lax.dot_general(left, right, (((1,), (1,)), ((), ())), preferred_element_type=F32)


def local_kernel(body, shapes, *args, scratch=()):
    return pl.pallas_call(
        body,
        out_shape=[jax.ShapeDtypeStruct(shape, dtype) for shape, dtype in shapes],
        in_specs=[pl.BlockSpec(memory_space=pltpu.VMEM)] * len(args),
        out_specs=[pl.BlockSpec(memory_space=pltpu.VMEM)] * len(shapes),
        scratch_shapes=list(scratch),
        compiler_params=pltpu.CompilerParams(vmem_limit_bytes=24 * 2**20),
        cost_estimate=pl.CostEstimate(flops=0, bytes_accessed=0, transcendentals=0),
    )(*args)


def load_body(*refs):
    half = (len(refs) - 1) // 2
    done = refs[-1]
    copies = [pltpu.make_async_copy(refs[i], refs[half + i], done.at[i]) for i in range(half)]
    for copy in copies:
        copy.start()
    for copy in copies:
        copy.wait()


def load(*args):
    return pl.pallas_call(
        load_body,
        out_shape=[jax.ShapeDtypeStruct(a.shape, a.dtype) for a in args],
        in_specs=[pl.BlockSpec(memory_space=pl.ANY)] * len(args),
        out_specs=[pl.BlockSpec(memory_space=pl.ANY)] * len(args),
        scratch_shapes=[pltpu.SemaphoreType.DMA((len(args),))],
        compiler_params=pltpu.CompilerParams(vmem_limit_bytes=16 * 2**20),
        cost_estimate=pl.CostEstimate(flops=0, bytes_accessed=0, transcendentals=0),
    )(*args)


def after(x, *earlier):
    return lax.optimization_barrier((x, *earlier))[0]


def fan_body(layer, cotangent, fan):
    for i in range(NZ):
        fan[i, 0] = layer[...]
        fan[i, 1] = cotangent[0]


def total_body(arrived, output, back):
    for kind, total in enumerate((output, back)):
        total[0] = sum(arrived[i, kind].astype(F32) for i in range(NZ)).astype(BF16)


def split_body(got_ref, own_ref):
    for kind in (0, 1):
        for pair in range(NZ // 2):
            two = [got_ref[2 * pair + i, kind].astype(F32) for i in (0, 1)]
            own_ref[kind, 8 * pair : 8 * pair + 8, :] = jnp.concatenate(two, 0).astype(BF16)


def put_sums(sums, columns, own, last, next_, step):
    own[:, columns] = sums[:32]
    last[:, columns] = sums[32:64].astype(BF16)
    next_[:, columns] = sums[64:96].astype(BF16)
    step[:, columns] = sums[96:].astype(BF16)


def forward_body(*refs):
    blocks, gate_ws, up_ws, down_ws = refs[:4], refs[4:6], refs[6:8], refs[8:10]
    hiddens, swish, rise, sends, layer = refs[10:12], refs[12], refs[13], refs[14:18], refs[18]
    for i, block in enumerate(blocks):
        layer[32 * i : 32 * i + 32, :] = block[0]
    for core in (0, 1):
        gate = jnp.dot(layer[...], gate_ws[core][0], preferred_element_type=F32)
        upper = jnp.dot(layer[...], up_ws[core][0], preferred_element_type=F32)
        sigma = jax.nn.sigmoid(gate)
        swish[core] = gate * sigma
        rise[core] = upper * (sigma * (1.0 + gate * (1.0 - sigma)))
        hiddens[core][...] = (swish[core] * upper).astype(BF16)

    @pl.loop(0, down_ws[0].shape[2], step=CHUNK)
    def _(start):
        columns = pl.ds(pl.multiple_of(start, CHUNK), CHUNK)
        sums = sum(
            jnp.dot(hiddens[core][...], down_ws[core][0, :, columns], preferred_element_type=F32) for core in (0, 1)
        )
        put_sums(sums, columns, *sends)


def turn_body(gate_w, up_w, gate_x, up_x, down_w, down_x, across, down):
    units = gate_w.shape[2]
    for i, source in enumerate((gate_w, up_w, gate_x, up_x)):

        @pl.loop(0, source.shape[1], step=CHUNK)
        def _(start):
            columns = pl.ds(pl.multiple_of(start, CHUNK), CHUNK)
            across[i * units : (i + 1) * units, columns] = source[0, columns, :].T

    for i, source in enumerate((down_w, down_x)):

        @pl.loop(0, source.shape[2], step=CHUNK)
        def _(start):
            columns = pl.ds(pl.multiple_of(start, CHUNK), CHUNK)
            down[columns, i * units : (i + 1) * units] = source[0, :, columns].T


def backward_body(*refs):
    blocks, across, down, (swish, rise, hidden) = refs[:4], refs[4], refs[5], refs[6:9]
    gate_grad, up_grad, give, sends, cotangent, grads = refs[9], refs[10], refs[11], refs[12:16], refs[16], refs[17]
    units = hidden.shape[1]
    give[2] = hidden[...]
    for i, block in enumerate(blocks):
        cotangent[32 * i : 32 * i + 32, :] = block[1]
    hidden_grads = jnp.dot(cotangent[...], down[...], preferred_element_type=F32)
    for core, (to_gate, to_up) in enumerate(((gate_grad, up_grad), (give.at[0], give.at[1]))):
        hidden_grad = hidden_grads[:, core * units : (core + 1) * units]
        to_gate[...] = (hidden_grad * rise[core]).astype(BF16)
        to_up[...] = (hidden_grad * swish[core]).astype(BF16)
        grads[:, 2 * core * units : (2 * core + 1) * units] = to_gate[...]
        grads[:, (2 * core + 1) * units : 2 * (core + 1) * units] = to_up[...]

    @pl.loop(0, across.shape[1], step=CHUNK)
    def _(start):
        columns = pl.ds(pl.multiple_of(start, CHUNK), CHUNK)
        put_sums(jnp.dot(grads[...], across[:, columns], preferred_element_type=F32), columns, *sends)


def weight_grads_body(*refs):
    blocks = refs[:8]
    gate_grad, up_grad, hidden = [(refs[8 + i], refs[11].at[i]) for i in range(3)]
    into_gate, into_up, into_down = refs[12:]
    layer = jnp.concatenate([block[0] for block in blocks], 0)
    for grad, into in ((gate_grad, into_gate), (up_grad, into_up)):
        grad = jnp.concatenate([grad[0][...], grad[1][...]], 0)
        into[0] = contract_rows(layer, grad).astype(BF16)
    hidden = jnp.concatenate([hidden[0][...], hidden[1][...]], 0)
    cotangent = jnp.concatenate([block[1] for block in blocks], 0)
    into_down[0] = contract_rows(hidden, cotangent).astype(BF16)


def weight_grads(*args):
    _, rows, width = args[0].shape
    tokens, units = args[8].shape
    part = width // 8
    streamed = [pl.BlockSpec((2, rows, part), lambda i: (0, 0, i))] * 8
    whole = [pl.BlockSpec((tokens, units), lambda i: (0, 0))] * 3 + [pl.BlockSpec((3, tokens, units), lambda i: (0, 0, 0))]
    across = [pl.BlockSpec((1, part, units), lambda i: (0, i, 0))] * 2
    along = [pl.BlockSpec((1, units, part), lambda i: (0, 0, i))]
    shapes = [(1, width, units), (1, width, units), (1, units, width)]
    return pl.pallas_call(
        weight_grads_body,
        grid=(width // part,),
        out_shape=[jax.ShapeDtypeStruct(shape, BF16) for shape in shapes],
        in_specs=streamed + whole,
        out_specs=across + along,
        compiler_params=pltpu.CompilerParams(vmem_limit_bytes=24 * 2**20),
        cost_estimate=pl.CostEstimate(flops=0, bytes_accessed=0, transcendentals=0),
    )(*args)


def add_terms(terms, joined, at):
    own, *received = terms
    for pair in range(NZ // 2):
        rows = slice(8 * pair, 8 * pair + 8)
        sums = own[rows, :]
        for term in received:
            sums = sums + term[rows, :].astype(F32)
        for i in (0, 1):
            joined[(2 * pair + i, *at)] = sums[4 * i : 4 * i + 4].astype(BF16)


def out_total_body(*refs):
    add_terms(refs[:4], refs[4], ())


def join_body(out_total, *refs):
    joined = refs[4]
    for i in range(NZ):
        joined[i, 0] = out_total[i]
    add_terms(refs[:4], joined, (1,))


def copy_body(source, target):
    target[...] = source[...]


def send_sums(own, last, next_, step):
    return [own, y_last(last), y_next(next_), z_step(step)]


def on_device(activations, w_gate, w_up, w_down, out_grad):
    arrived = from_behind(activations[0], "section", 1)
    rows, width = arrived.shape
    units = w_down.shape[1]
    tokens = NY * NZ * rows
    (out_grad,) = local_kernel(copy_body, [(out_grad.shape, BF16)], out_grad)
    (mine,) = local_kernel(fan_body, [((NZ, 2, rows, width), BF16)], arrived, out_grad)
    got = colour_all_to_all(mine)

    got, *partner = lax.optimization_barrier((got, swap(w_gate), swap(w_up), swap(w_down)))

    (own,) = local_kernel(split_body, [((2, NZ * rows, width), BF16)], got)
    next_, last, step = y_next(own), y_last(own), z_step(own)
    loaded = load(after(w_gate, own), w_up, w_down)
    weights = [w for pair in zip(loaded, partner) for w in pair]
    turned = local_kernel(
        turn_body, [((4 * units, width), BF16), ((width, 2 * units), BF16)],
        loaded[0], loaded[1], partner[0], partner[1], loaded[2], partner[2])
    next_, last = lax.optimization_barrier((next_, last, *turned))[:2]
    blocks = [own, next_, last, step]

    send = ((NZ * rows, width), BF16)
    sends = [((NZ * rows, width), F32), send, send, send]
    some = ((tokens, units), BF16)
    scratch = [pltpu.VMEM((tokens, width), BF16)]
    kept = ((2, tokens, units), F32)
    hidden, hidden_other, swish, rise, *out_sums = local_kernel(
        forward_body, [some, some, kept, kept, *sends], *blocks, *weights, scratch=scratch)
    out_terms = send_sums(*out_sums)
    gate_grad, up_grad, give, *back_sums = local_kernel(
        backward_body, [some, some, ((3, tokens, units), BF16), *sends],
        *blocks, *turned, swish, rise, hidden_other,
        scratch=scratch + [pltpu.VMEM((tokens, 4 * units), BF16)])
    back_terms = send_sums(*back_sums)

    (out_total,) = local_kernel(out_total_body, [((NZ, rows, width), BF16)], *out_terms)
    (sums,) = local_kernel(join_body, [((NZ, 2, rows, width), BF16)], out_total, *back_terms)

    *blocks, give = lax.optimization_barrier((*blocks, give, sums))[:-1]
    grad_gate, grad_up, grad_down = weight_grads(
        *blocks, *[swap(block) for block in blocks], gate_grad, up_grad, hidden, swap(give))
    arrived = colour_all_to_all(sums)
    arrived, grad_gate, grad_up, grad_down = lax.optimization_barrier((arrived, grad_gate, grad_up, grad_down))
    output, back = local_kernel(total_body, [((1, rows, width), BF16)] * 2, arrived)
    return (output, from_behind(back, "section", -1), grad_gate, grad_up, grad_down)


def solution(mesh):
    return jax.shard_map(
        on_device,
        mesh=mesh,
        in_specs=(
            P("section", PLANE, None),
            P("section", None, PLANE),
            P("section", None, PLANE),
            P("section", PLANE, None),
            P("section", PLANE, None),
        ),
        out_specs=(
            P("section", PLANE, None),
            P("section", PLANE, None),
            P("section", None, PLANE),
            P("section", None, PLANE),
            P("section", PLANE, None),
        ),
        check_vma=False,
    )
```

```python
import functools

import jax
import jax.numpy as jnp
from jax import lax
from jax.experimental import pallas as pl
from jax.experimental.pallas import tpu as pltpu
from jax.sharding import PartitionSpec as P

PLANE = ("dp", "tensor")
NY, NZ = 4, 8
BF16 = jnp.bfloat16
F32 = jnp.float32
CHUNK = 4096


def place(y, z, core):
    y, z = y % NY, z % NZ
    return ((y * 2 + z % 2) * 4 + z // 2) * 2 + core


CHIPS = [(y, z) for y in range(NY) for z in range(NZ)]
CORE_SWAP = [(place(y, z, c), place(y, z, 1 - c)) for y, z in CHIPS for c in (0, 1)]
Y_NEXT = [(place(y, z, c), place(y + 1, z, c)) for y, z in CHIPS for c in (0, 1)]
Y_LAST = [(place(y, z, c), place(y - 1, z, c)) for y, z in CHIPS for c in (0, 1)]
Z_STEP = [(place(y, z, c), place(y, z + 1 - 2 * c, c)) for y, z in CHIPS for c in (0, 1)]
COLOURS = [[place(k - 2 * z, z, c) for z in range(NZ)] for k in range(NY) for c in (0, 1)]


def swap(x):
    return lax.ppermute(x, PLANE, CORE_SWAP)


def y_next(x):
    return lax.ppermute(x, PLANE, Y_NEXT)


def y_last(x):
    return lax.ppermute(x, PLANE, Y_LAST)


def z_step(x):
    return lax.ppermute(x, PLANE, Z_STEP)


def colour_all_to_all(x):
    return lax.all_to_all(x, PLANE, 0, 0, axis_index_groups=COLOURS)


def from_behind(x, axis, by):
    length = lax.axis_size(axis)
    return lax.ppermute(x, axis, [(i, (i + by) % length) for i in range(length)])


def contract_rows(left, right):
    return lax.dot_general(left, right, (((0,), (0,)), ((), ())), preferred_element_type=F32)


def contract_cols(left, right):
    return lax.dot_general(left, right, (((1,), (1,)), ((), ())), preferred_element_type=F32)


def local_kernel(body, shapes, *args, scratch=()):
    return pl.pallas_call(
        body,
        out_shape=[jax.ShapeDtypeStruct(shape, dtype) for shape, dtype in shapes],
        in_specs=[pl.BlockSpec(memory_space=pltpu.VMEM)] * len(args),
        out_specs=[pl.BlockSpec(memory_space=pltpu.VMEM)] * len(shapes),
        scratch_shapes=list(scratch),
        compiler_params=pltpu.CompilerParams(vmem_limit_bytes=24 * 2**20),
        cost_estimate=pl.CostEstimate(flops=0, bytes_accessed=0, transcendentals=0),
    )(*args)


def load_body(*refs):
    half = (len(refs) - 1) // 2
    done = refs[-1]
    copies = [pltpu.make_async_copy(refs[i], refs[half + i], done.at[i]) for i in range(half)]
    for copy in copies:
        copy.start()
    for copy in copies:
        copy.wait()


def load(*args):
    return pl.pallas_call(
        load_body,
        out_shape=[jax.ShapeDtypeStruct(a.shape, a.dtype) for a in args],
        in_specs=[pl.BlockSpec(memory_space=pl.ANY)] * len(args),
        out_specs=[pl.BlockSpec(memory_space=pl.ANY)] * len(args),
        scratch_shapes=[pltpu.SemaphoreType.DMA((len(args),))],
        compiler_params=pltpu.CompilerParams(vmem_limit_bytes=16 * 2**20),
        cost_estimate=pl.CostEstimate(flops=0, bytes_accessed=0, transcendentals=0),
    )(*args)


def after(x, *earlier):
    return lax.optimization_barrier((x, *earlier))[0]


def fan_body(layer, cotangent, fan):
    for i in range(NZ):
        fan[i, 0] = layer[...]
        fan[i, 1] = cotangent[0]


def total_body(kind, arrived, total):
    total[0] = sum(arrived[i, kind].astype(F32) for i in range(NZ)).astype(BF16)


def split_body(got_ref, own_ref):
    for kind in (0, 1):
        for pair in range(NZ // 2):
            two = [got_ref[2 * pair + i, kind].astype(F32) for i in (0, 1)]
            own_ref[kind, 8 * pair : 8 * pair + 8, :] = jnp.concatenate(two, 0).astype(BF16)


def put_sums(sums, columns, own, last, next_, step):
    own[:, columns] = sums[:32]
    last[:, columns] = sums[32:64].astype(BF16)
    next_[:, columns] = sums[64:96].astype(BF16)
    step[:, columns] = sums[96:].astype(BF16)


def forward_body(*refs):
    blocks, gate_ws, up_ws, down_ws = refs[:4], refs[4:6], refs[6:8], refs[8:10]
    hiddens, swish, rise, sends, layer = refs[10:12], refs[12], refs[13], refs[14:18], refs[18]
    for i, block in enumerate(blocks):
        layer[32 * i : 32 * i + 32, :] = block[0]
    for core in (0, 1):
        gate = jnp.dot(layer[...], gate_ws[core][0], preferred_element_type=F32)
        upper = jnp.dot(layer[...], up_ws[core][0], preferred_element_type=F32)
        sigma = jax.nn.sigmoid(gate)
        swish[core] = gate * sigma
        rise[core] = upper * (sigma * (1.0 + gate * (1.0 - sigma)))
        hiddens[core][...] = (swish[core] * upper).astype(BF16)

    @pl.loop(0, down_ws[0].shape[2], step=CHUNK)
    def _(start):
        columns = pl.ds(pl.multiple_of(start, CHUNK), CHUNK)
        sums = sum(
            jnp.dot(hiddens[core][...], down_ws[core][0, :, columns], preferred_element_type=F32) for core in (0, 1)
        )
        put_sums(sums, columns, *sends)


def turn_body(gate_w, up_w, gate_x, up_x, down_w, down_x, across, down):
    units = gate_w.shape[2]
    for i, source in enumerate((gate_w, up_w, gate_x, up_x)):

        @pl.loop(0, source.shape[1], step=CHUNK)
        def _(start):
            columns = pl.ds(pl.multiple_of(start, CHUNK), CHUNK)
            across[i * units : (i + 1) * units, columns] = source[0, columns, :].T

    for i, source in enumerate((down_w, down_x)):

        @pl.loop(0, source.shape[2], step=CHUNK)
        def _(start):
            columns = pl.ds(pl.multiple_of(start, CHUNK), CHUNK)
            down[columns, i * units : (i + 1) * units] = source[0, :, columns].T


def backward_body(*refs):
    blocks, across, down, (swish, rise, hidden) = refs[:4], refs[4], refs[5], refs[6:9]
    gate_grad, up_grad, give, sends, cotangent, grads = refs[9], refs[10], refs[11], refs[12:16], refs[16], refs[17]
    units = hidden.shape[1]
    give[2] = hidden[...]
    for i, block in enumerate(blocks):
        cotangent[32 * i : 32 * i + 32, :] = block[1]
    hidden_grads = jnp.dot(cotangent[...], down[...], preferred_element_type=F32)
    for core, (to_gate, to_up) in enumerate(((gate_grad, up_grad), (give.at[0], give.at[1]))):
        hidden_grad = hidden_grads[:, core * units : (core + 1) * units]
        to_gate[...] = (hidden_grad * rise[core]).astype(BF16)
        to_up[...] = (hidden_grad * swish[core]).astype(BF16)
        grads[:, 2 * core * units : (2 * core + 1) * units] = to_gate[...]
        grads[:, (2 * core + 1) * units : 2 * (core + 1) * units] = to_up[...]

    @pl.loop(0, across.shape[1], step=CHUNK)
    def _(start):
        columns = pl.ds(pl.multiple_of(start, CHUNK), CHUNK)
        put_sums(jnp.dot(grads[...], across[:, columns], preferred_element_type=F32), columns, *sends)


def weight_grads_body(*refs):
    blocks = refs[:8]
    gate_grad, up_grad, hidden = [(refs[8 + i], refs[11].at[i]) for i in range(3)]
    into_gate, into_up, into_down = refs[12:]
    layer = jnp.concatenate([block[0] for block in blocks], 0)
    for grad, into in ((gate_grad, into_gate), (up_grad, into_up)):
        grad = jnp.concatenate([grad[0][...], grad[1][...]], 0)
        into[0] = contract_rows(layer, grad).astype(BF16)
    hidden = jnp.concatenate([hidden[0][...], hidden[1][...]], 0)
    cotangent = jnp.concatenate([block[1] for block in blocks], 0)
    into_down[0] = contract_rows(hidden, cotangent).astype(BF16)


def weight_grads(*args):
    _, rows, width = args[0].shape
    tokens, units = args[8].shape
    part = width // 4
    streamed = [pl.BlockSpec((2, rows, part), lambda i: (0, 0, i))] * 8
    whole = [pl.BlockSpec((tokens, units), lambda i: (0, 0))] * 3 + [pl.BlockSpec((3, tokens, units), lambda i: (0, 0, 0))]
    across = [pl.BlockSpec((1, part, units), lambda i: (0, i, 0))] * 2
    along = [pl.BlockSpec((1, units, part), lambda i: (0, 0, i))]
    shapes = [(1, width, units), (1, width, units), (1, units, width)]
    return pl.pallas_call(
        weight_grads_body,
        grid=(width // part,),
        out_shape=[jax.ShapeDtypeStruct(shape, BF16) for shape in shapes],
        in_specs=streamed + whole,
        out_specs=across + along,
        compiler_params=pltpu.CompilerParams(vmem_limit_bytes=24 * 2**20),
        cost_estimate=pl.CostEstimate(flops=0, bytes_accessed=0, transcendentals=0),
    )(*args)


def add_terms(terms, joined, at):
    own, *received = terms
    for pair in range(NZ // 2):
        rows = slice(8 * pair, 8 * pair + 8)
        sums = own[rows, :]
        for term in received:
            sums = sums + term[rows, :].astype(F32)
        for i in (0, 1):
            joined[(2 * pair + i, *at)] = sums[4 * i : 4 * i + 4].astype(BF16)


def out_total_body(*refs):
    add_terms(refs[:4], refs[4], ())


def join_body(out_total, *refs):
    joined = refs[4]
    for i in range(NZ):
        joined[i, 0] = out_total[i]
    add_terms(refs[:4], joined, (1,))


def copy_body(source, target):
    target[...] = source[...]


def send_sums(own, last, next_, step):
    return [own, y_last(last), y_next(next_), z_step(step)]


def on_device(activations, w_gate, w_up, w_down, out_grad):
    arrived = from_behind(activations[0], "section", 1)
    rows, width = arrived.shape
    units = w_down.shape[1]
    tokens = NY * NZ * rows
    (out_grad,) = local_kernel(copy_body, [(out_grad.shape, BF16)], out_grad)
    (mine,) = local_kernel(fan_body, [((NZ, 2, rows, width), BF16)], arrived, out_grad)
    got = colour_all_to_all(mine)

    got, *partner = lax.optimization_barrier((got, swap(w_gate), swap(w_up), swap(w_down)))

    (own,) = local_kernel(split_body, [((2, NZ * rows, width), BF16)], got)
    next_, last, step = y_next(own), y_last(own), z_step(own)
    loaded = load(after(w_gate, own), w_up, w_down)
    weights = [w for pair in zip(loaded, partner) for w in pair]
    turned = local_kernel(
        turn_body, [((4 * units, width), BF16), ((width, 2 * units), BF16)],
        loaded[0], loaded[1], partner[0], partner[1], loaded[2], partner[2])
    next_, last = lax.optimization_barrier((next_, last, *turned))[:2]
    blocks = [own, next_, last, step]

    send = ((NZ * rows, width), BF16)
    sends = [((NZ * rows, width), F32), send, send, send]
    some = ((tokens, units), BF16)
    scratch = [pltpu.VMEM((tokens, width), BF16)]
    kept = ((2, tokens, units), F32)
    hidden, hidden_other, swish, rise, *out_sums = local_kernel(
        forward_body, [some, some, kept, kept, *sends], *blocks, *weights, scratch=scratch)
    out_terms = send_sums(*out_sums)
    gate_grad, up_grad, give, *back_sums = local_kernel(
        backward_body, [some, some, ((3, tokens, units), BF16), *sends],
        *blocks, *turned, swish, rise, hidden_other,
        scratch=scratch + [pltpu.VMEM((tokens, 4 * units), BF16)])
    back_terms = send_sums(*back_sums)

    (out_total,) = local_kernel(out_total_body, [((NZ, rows, width), BF16)], *out_terms)
    (sums,) = local_kernel(join_body, [((NZ, 2, rows, width), BF16)], out_total, *back_terms)

    *blocks, give = lax.optimization_barrier((*blocks, give, sums))[:-1]
    grad_gate, grad_up, grad_down = weight_grads(
        *blocks, *[swap(block) for block in blocks], gate_grad, up_grad, hidden, swap(give))
    arrived = colour_all_to_all(sums)
    arrived, grad_gate, grad_up, grad_down = lax.optimization_barrier((arrived, grad_gate, grad_up, grad_down))
    total = ((1, rows, width), BF16)
    (back,) = local_kernel(functools.partial(total_body, 1), [total], arrived)
    returned = from_behind(back, "section", -1)
    (output,) = local_kernel(functools.partial(total_body, 0), [total], arrived)
    return (output, returned, grad_gate, grad_up, grad_down)


def solution(mesh):
    return jax.shard_map(
        on_device,
        mesh=mesh,
        in_specs=(
            P("section", PLANE, None),
            P("section", None, PLANE),
            P("section", None, PLANE),
            P("section", PLANE, None),
            P("section", PLANE, None),
        ),
        out_specs=(
            P("section", PLANE, None),
            P("section", PLANE, None),
            P("section", None, PLANE),
            P("section", None, PLANE),
            P("section", PLANE, None),
        ),
        check_vma=False,
    )
```

```python
import functools

import jax
import jax.numpy as jnp
from jax import lax
from jax.experimental import pallas as pl
from jax.experimental.pallas import tpu as pltpu
from jax.sharding import PartitionSpec as P

PLANE = ("dp", "tensor")
NY, NZ = 4, 8
BF16 = jnp.bfloat16
F32 = jnp.float32
CHUNK = 4096


def place(y, z, core):
    y, z = y % NY, z % NZ
    return ((y * 2 + z % 2) * 4 + z // 2) * 2 + core


CHIPS = [(y, z) for y in range(NY) for z in range(NZ)]
CORE_SWAP = [(place(y, z, c), place(y, z, 1 - c)) for y, z in CHIPS for c in (0, 1)]
Y_NEXT = [(place(y, z, c), place(y + 1, z, c)) for y, z in CHIPS for c in (0, 1)]
Y_LAST = [(place(y, z, c), place(y - 1, z, c)) for y, z in CHIPS for c in (0, 1)]
Z_STEP = [(place(y, z, c), place(y, z + 1 - 2 * c, c)) for y, z in CHIPS for c in (0, 1)]
COLOURS = [[place(k - 2 * z, z, c) for z in range(NZ)] for k in range(NY) for c in (0, 1)]


def swap(x):
    return lax.ppermute(x, PLANE, CORE_SWAP)


def y_next(x):
    return lax.ppermute(x, PLANE, Y_NEXT)


def y_last(x):
    return lax.ppermute(x, PLANE, Y_LAST)


def z_step(x):
    return lax.ppermute(x, PLANE, Z_STEP)


def colour_all_to_all(x):
    return lax.all_to_all(x, PLANE, 0, 0, axis_index_groups=COLOURS)


def from_behind(x, axis, by):
    length = lax.axis_size(axis)
    return lax.ppermute(x, axis, [(i, (i + by) % length) for i in range(length)])


def contract_rows(left, right):
    return lax.dot_general(left, right, (((0,), (0,)), ((), ())), preferred_element_type=F32)


def contract_cols(left, right):
    return lax.dot_general(left, right, (((1,), (1,)), ((), ())), preferred_element_type=F32)


def local_kernel(body, shapes, *args, scratch=()):
    return pl.pallas_call(
        body,
        out_shape=[jax.ShapeDtypeStruct(shape, dtype) for shape, dtype in shapes],
        in_specs=[pl.BlockSpec(memory_space=pltpu.VMEM)] * len(args),
        out_specs=[pl.BlockSpec(memory_space=pltpu.VMEM)] * len(shapes),
        scratch_shapes=list(scratch),
        compiler_params=pltpu.CompilerParams(vmem_limit_bytes=24 * 2**20),
        cost_estimate=pl.CostEstimate(flops=0, bytes_accessed=0, transcendentals=0),
    )(*args)


def load_body(*refs):
    half = (len(refs) - 1) // 2
    done = refs[-1]
    copies = [pltpu.make_async_copy(refs[i], refs[half + i], done.at[i]) for i in range(half)]
    for copy in copies:
        copy.start()
    for copy in copies:
        copy.wait()


def load(*args):
    return pl.pallas_call(
        load_body,
        out_shape=[jax.ShapeDtypeStruct(a.shape, a.dtype) for a in args],
        in_specs=[pl.BlockSpec(memory_space=pl.ANY)] * len(args),
        out_specs=[pl.BlockSpec(memory_space=pl.ANY)] * len(args),
        scratch_shapes=[pltpu.SemaphoreType.DMA((len(args),))],
        compiler_params=pltpu.CompilerParams(vmem_limit_bytes=16 * 2**20),
        cost_estimate=pl.CostEstimate(flops=0, bytes_accessed=0, transcendentals=0),
    )(*args)


def after(x, *earlier):
    return lax.optimization_barrier((x, *earlier))[0]


def fan_body(layer, cotangent, fan):
    for i in range(NZ):
        fan[i, 0] = layer[...]
        fan[i, 1] = cotangent[0]


def total_body(kind, arrived, total):
    total[0] = sum(arrived[i, kind].astype(F32) for i in range(NZ)).astype(BF16)


def split_body(got_ref, own_ref):
    for kind in (0, 1):
        for half in (0, 1):
            four = [got_ref[4 * half + i, kind].astype(F32) for i in range(4)]
            own_ref[kind, 16 * half : 16 * half + 16, :] = jnp.concatenate(four, 0).astype(BF16)


def put_sums(sums, columns, own, last, next_, step):
    own[:, columns] = sums[:32]
    last[:, columns] = sums[32:64].astype(BF16)
    next_[:, columns] = sums[64:96].astype(BF16)
    step[:, columns] = sums[96:].astype(BF16)


def forward_body(*refs):
    blocks, gate_ws, up_ws, down_ws = refs[:4], refs[4:6], refs[6:8], refs[8:10]
    hiddens, swish, rise, sends, layer = refs[10:12], refs[12], refs[13], refs[14:18], refs[18]
    for i, block in enumerate(blocks):
        layer[32 * i : 32 * i + 32, :] = block[0]
    for core in (0, 1):
        gate = jnp.dot(layer[...], gate_ws[core][0], preferred_element_type=F32)
        upper = jnp.dot(layer[...], up_ws[core][0], preferred_element_type=F32)
        sigma = jax.nn.sigmoid(gate)
        swish[core] = gate * sigma
        rise[core] = upper * (sigma * (1.0 + gate * (1.0 - sigma)))
        hiddens[core][...] = (swish[core] * upper).astype(BF16)

    @pl.loop(0, down_ws[0].shape[2], step=CHUNK)
    def _(start):
        columns = pl.ds(pl.multiple_of(start, CHUNK), CHUNK)
        sums = sum(
            jnp.dot(hiddens[core][...], down_ws[core][0, :, columns], preferred_element_type=F32) for core in (0, 1)
        )
        put_sums(sums, columns, *sends)


def turn_body(gate_w, up_w, gate_x, up_x, down_w, down_x, across, down):
    units = gate_w.shape[2]
    for i, source in enumerate((gate_w, up_w, gate_x, up_x)):

        @pl.loop(0, source.shape[1], step=CHUNK)
        def _(start):
            columns = pl.ds(pl.multiple_of(start, CHUNK), CHUNK)
            across[i * units : (i + 1) * units, columns] = source[0, columns, :].T

    for i, source in enumerate((down_w, down_x)):

        @pl.loop(0, source.shape[2], step=CHUNK)
        def _(start):
            columns = pl.ds(pl.multiple_of(start, CHUNK), CHUNK)
            down[columns, i * units : (i + 1) * units] = source[0, :, columns].T


def backward_body(*refs):
    blocks, across, down, (swish, rise, hidden) = refs[:4], refs[4], refs[5], refs[6:9]
    gate_grad, up_grad, give, sends, cotangent, grads = refs[9], refs[10], refs[11], refs[12:16], refs[16], refs[17]
    units = hidden.shape[1]
    give[2] = hidden[...]
    for i, block in enumerate(blocks):
        cotangent[32 * i : 32 * i + 32, :] = block[1]
    hidden_grads = jnp.dot(cotangent[...], down[...], preferred_element_type=F32)
    for core, (to_gate, to_up) in enumerate(((gate_grad, up_grad), (give.at[0], give.at[1]))):
        hidden_grad = hidden_grads[:, core * units : (core + 1) * units]
        to_gate[...] = (hidden_grad * rise[core]).astype(BF16)
        to_up[...] = (hidden_grad * swish[core]).astype(BF16)
        grads[:, 2 * core * units : (2 * core + 1) * units] = to_gate[...]
        grads[:, (2 * core + 1) * units : 2 * (core + 1) * units] = to_up[...]

    @pl.loop(0, across.shape[1], step=CHUNK)
    def _(start):
        columns = pl.ds(pl.multiple_of(start, CHUNK), CHUNK)
        put_sums(jnp.dot(grads[...], across[:, columns], preferred_element_type=F32), columns, *sends)


def weight_grads_body(*refs):
    blocks = refs[:8]
    gate_grad, up_grad, hidden = [(refs[8 + i], refs[11].at[i]) for i in range(3)]
    into_gate, into_up, into_down = refs[12:]
    layer = jnp.concatenate([block[0] for block in blocks], 0)
    for grad, into in ((gate_grad, into_gate), (up_grad, into_up)):
        grad = jnp.concatenate([grad[0][...], grad[1][...]], 0)
        into[0] = contract_rows(layer, grad).astype(BF16)
    hidden = jnp.concatenate([hidden[0][...], hidden[1][...]], 0)
    cotangent = jnp.concatenate([block[1] for block in blocks], 0)
    into_down[0] = contract_rows(hidden, cotangent).astype(BF16)


def weight_grads(*args):
    _, rows, width = args[0].shape
    tokens, units = args[8].shape
    part = width // 4
    streamed = [pl.BlockSpec((2, rows, part), lambda i: (0, 0, i))] * 8
    whole = [pl.BlockSpec((tokens, units), lambda i: (0, 0))] * 3 + [pl.BlockSpec((3, tokens, units), lambda i: (0, 0, 0))]
    across = [pl.BlockSpec((1, part, units), lambda i: (0, i, 0))] * 2
    along = [pl.BlockSpec((1, units, part), lambda i: (0, 0, i))]
    shapes = [(1, width, units), (1, width, units), (1, units, width)]
    return pl.pallas_call(
        weight_grads_body,
        grid=(width // part,),
        out_shape=[jax.ShapeDtypeStruct(shape, BF16) for shape in shapes],
        in_specs=streamed + whole,
        out_specs=across + along,
        compiler_params=pltpu.CompilerParams(vmem_limit_bytes=24 * 2**20),
        cost_estimate=pl.CostEstimate(flops=0, bytes_accessed=0, transcendentals=0),
    )(*args)


def add_terms(terms, joined, at):
    own, *received = terms
    for half in (0, 1):
        rows = slice(16 * half, 16 * half + 16)
        sums = own[rows, :]
        for term in received:
            sums = sums + term[rows, :].astype(F32)
        for i in range(4):
            joined[(4 * half + i, *at)] = sums[4 * i : 4 * i + 4].astype(BF16)


def out_total_body(*refs):
    add_terms(refs[:4], refs[4], ())


def join_body(out_total, *refs):
    joined = refs[4]
    for i in range(NZ):
        joined[i, 0] = out_total[i]
    add_terms(refs[:4], joined, (1,))


def copy_body(source, target):
    target[...] = source[...]


def send_sums(own, last, next_, step):
    return [own, y_last(last), y_next(next_), z_step(step)]


def on_device(activations, w_gate, w_up, w_down, out_grad):
    arrived = from_behind(activations[0], "section", 1)
    rows, width = arrived.shape
    units = w_down.shape[1]
    tokens = NY * NZ * rows
    (out_grad,) = local_kernel(copy_body, [(out_grad.shape, BF16)], out_grad)
    (mine,) = local_kernel(fan_body, [((NZ, 2, rows, width), BF16)], arrived, out_grad)
    got = colour_all_to_all(mine)

    got, *partner = lax.optimization_barrier((got, swap(w_gate), swap(w_up), swap(w_down)))

    (own,) = local_kernel(split_body, [((2, NZ * rows, width), BF16)], got)
    next_, last, step = y_next(own), y_last(own), z_step(own)
    loaded = load(after(w_gate, own), w_up, w_down)
    weights = [w for pair in zip(loaded, partner) for w in pair]
    turned = local_kernel(
        turn_body, [((4 * units, width), BF16), ((width, 2 * units), BF16)],
        loaded[0], loaded[1], partner[0], partner[1], loaded[2], partner[2])
    next_, last = lax.optimization_barrier((next_, last, *turned))[:2]
    blocks = [own, next_, last, step]

    send = ((NZ * rows, width), BF16)
    sends = [((NZ * rows, width), F32), send, send, send]
    some = ((tokens, units), BF16)
    scratch = [pltpu.VMEM((tokens, width), BF16)]
    kept = ((2, tokens, units), F32)
    hidden, hidden_other, swish, rise, *out_sums = local_kernel(
        forward_body, [some, some, kept, kept, *sends], *blocks, *weights, scratch=scratch)
    out_terms = send_sums(*out_sums)
    gate_grad, up_grad, give, *back_sums = local_kernel(
        backward_body, [some, some, ((3, tokens, units), BF16), *sends],
        *blocks, *turned, swish, rise, hidden_other,
        scratch=scratch + [pltpu.VMEM((tokens, 4 * units), BF16)])
    back_terms = send_sums(*back_sums)

    (out_total,) = local_kernel(out_total_body, [((NZ, rows, width), BF16)], *out_terms)
    (sums,) = local_kernel(join_body, [((NZ, 2, rows, width), BF16)], out_total, *back_terms)

    *blocks, give = lax.optimization_barrier((*blocks, give, sums))[:-1]
    grad_gate, grad_up, grad_down = weight_grads(
        *blocks, *[swap(block) for block in blocks], gate_grad, up_grad, hidden, swap(give))
    arrived = colour_all_to_all(sums)
    arrived, grad_gate, grad_up, grad_down = lax.optimization_barrier((arrived, grad_gate, grad_up, grad_down))
    total = ((1, rows, width), BF16)
    (back,) = local_kernel(functools.partial(total_body, 1), [total], arrived)
    returned = from_behind(back, "section", -1)
    (output,) = local_kernel(functools.partial(total_body, 0), [total], arrived)
    return (output, returned, grad_gate, grad_up, grad_down)


def solution(mesh):
    return jax.shard_map(
        on_device,
        mesh=mesh,
        in_specs=(
            P("section", PLANE, None),
            P("section", None, PLANE),
            P("section", None, PLANE),
            P("section", PLANE, None),
            P("section", PLANE, None),
        ),
        out_specs=(
            P("section", PLANE, None),
            P("section", PLANE, None),
            P("section", None, PLANE),
            P("section", None, PLANE),
            P("section", PLANE, None),
        ),
        check_vma=False,
    )
```

```python
import functools

import jax
import jax.numpy as jnp
from jax import lax
from jax.experimental import pallas as pl
from jax.experimental.pallas import tpu as pltpu
from jax.sharding import PartitionSpec as P

PLANE = ("dp", "tensor")
NY, NZ = 4, 8
BF16 = jnp.bfloat16
F32 = jnp.float32


def place(y, z, core):
    y, z = y % NY, z % NZ
    return ((y * 2 + z % 2) * 4 + z // 2) * 2 + core


CHIPS = [(y, z) for y in range(NY) for z in range(NZ)]
CORE_SWAP = [(place(y, z, c), place(y, z, 1 - c)) for y, z in CHIPS for c in (0, 1)]
Y_NEXT = [(place(y, z, c), place(y + 1, z, c)) for y, z in CHIPS for c in (0, 1)]
Y_LAST = [(place(y, z, c), place(y - 1, z, c)) for y, z in CHIPS for c in (0, 1)]
Z_STEP = [(place(y, z, c), place(y, z + 1 - 2 * c, c)) for y, z in CHIPS for c in (0, 1)]
COLOURS = [[place(k - 2 * z, z, c) for z in range(NZ)] for k in range(NY) for c in (0, 1)]


def swap(x):
    return lax.ppermute(x, PLANE, CORE_SWAP)


def y_next(x):
    return lax.ppermute(x, PLANE, Y_NEXT)


def y_last(x):
    return lax.ppermute(x, PLANE, Y_LAST)


def z_step(x):
    return lax.ppermute(x, PLANE, Z_STEP)


def colour_all_to_all(x):
    return lax.all_to_all(x, PLANE, 0, 0, axis_index_groups=COLOURS)


def from_behind(x, axis, by):
    length = lax.axis_size(axis)
    return lax.ppermute(x, axis, [(i, (i + by) % length) for i in range(length)])


def contract_rows(left, right):
    return lax.dot_general(left, right, (((0,), (0,)), ((), ())), preferred_element_type=F32)


def contract_cols(left, right):
    return lax.dot_general(left, right, (((1,), (1,)), ((), ())), preferred_element_type=F32)


def local_kernel(body, shapes, *args, scratch=()):
    return pl.pallas_call(
        body,
        out_shape=[jax.ShapeDtypeStruct(shape, dtype) for shape, dtype in shapes],
        in_specs=[pl.BlockSpec(memory_space=pltpu.VMEM)] * len(args),
        out_specs=[pl.BlockSpec(memory_space=pltpu.VMEM)] * len(shapes),
        scratch_shapes=list(scratch),
        compiler_params=pltpu.CompilerParams(vmem_limit_bytes=24 * 2**20),
        cost_estimate=pl.CostEstimate(flops=0, bytes_accessed=0, transcendentals=0),
    )(*args)


def load_body(*refs):
    half = (len(refs) - 1) // 2
    done = refs[-1]
    copies = [pltpu.make_async_copy(refs[i], refs[half + i], done.at[i]) for i in range(half)]
    for copy in copies:
        copy.start()
    for copy in copies:
        copy.wait()


def load(*args):
    return pl.pallas_call(
        load_body,
        out_shape=[jax.ShapeDtypeStruct(a.shape, a.dtype) for a in args],
        in_specs=[pl.BlockSpec(memory_space=pl.ANY)] * len(args),
        out_specs=[pl.BlockSpec(memory_space=pl.ANY)] * len(args),
        scratch_shapes=[pltpu.SemaphoreType.DMA((len(args),))],
        compiler_params=pltpu.CompilerParams(vmem_limit_bytes=16 * 2**20),
        cost_estimate=pl.CostEstimate(flops=0, bytes_accessed=0, transcendentals=0),
    )(*args)


def after(x, *earlier):
    return lax.optimization_barrier((x, *earlier))[0]


def fan_body(layer, cotangent, fan):
    for i in range(NZ):
        fan[i, 0] = layer[...]
        fan[i, 1] = cotangent[0]


def total_body(kind, arrived, total):
    total[0] = sum(arrived[i, kind].astype(F32) for i in range(NZ)).astype(BF16)


def split_body(got_ref, own_ref):
    for kind in (0, 1):
        for half in (0, 1):
            four = [got_ref[4 * half + i, kind].astype(F32) for i in range(4)]
            own_ref[kind, 16 * half : 16 * half + 16, :] = jnp.concatenate(four, 0).astype(BF16)


def put_sums(sums, columns, own, last, next_, step):
    own[:, columns] = sums[:32]
    last[:, columns] = sums[32:64].astype(BF16)
    next_[:, columns] = sums[64:96].astype(BF16)
    step[:, columns] = sums[96:].astype(BF16)


def forward_body(*refs):
    blocks, gate_ws, up_ws, down_ws = refs[:4], refs[4:6], refs[6:8], refs[8:10]
    hiddens, swish, rise, sends, layer = refs[10:12], refs[12], refs[13], refs[14:18], refs[18]
    for i, block in enumerate(blocks):
        layer[32 * i : 32 * i + 32, :] = block[0]
    for core in (0, 1):
        gate = jnp.dot(layer[...], gate_ws[core][0], preferred_element_type=F32)
        upper = jnp.dot(layer[...], up_ws[core][0], preferred_element_type=F32)
        sigma = jax.nn.sigmoid(gate)
        swish[core] = gate * sigma
        rise[core] = upper * (sigma * (1.0 + gate * (1.0 - sigma)))
        hiddens[core][...] = (swish[core] * upper).astype(BF16)

    columns = slice(None)
    sums = sum(
        jnp.dot(hiddens[core][...], down_ws[core][0, :, columns], preferred_element_type=F32) for core in (0, 1)
    )
    put_sums(sums, columns, *sends)


def turn_body(gate_w, up_w, gate_x, up_x, down_w, down_x, across, down):
    units = gate_w.shape[2]
    for i, source in enumerate((gate_w, up_w, gate_x, up_x)):

        columns = slice(None)
        across[i * units : (i + 1) * units, columns] = source[0, columns, :].T

    for i, source in enumerate((down_w, down_x)):

        columns = slice(None)
        down[columns, i * units : (i + 1) * units] = source[0, :, columns].T


def backward_body(*refs):
    blocks, across, down, (swish, rise, hidden) = refs[:4], refs[4], refs[5], refs[6:9]
    gate_grad, up_grad, give, sends, cotangent, grads = refs[9], refs[10], refs[11], refs[12:16], refs[16], refs[17]
    units = hidden.shape[1]
    give[2] = hidden[...]
    for i, block in enumerate(blocks):
        cotangent[32 * i : 32 * i + 32, :] = block[1]
    hidden_grads = jnp.dot(cotangent[...], down[...], preferred_element_type=F32)
    for core, (to_gate, to_up) in enumerate(((gate_grad, up_grad), (give.at[0], give.at[1]))):
        hidden_grad = hidden_grads[:, core * units : (core + 1) * units]
        to_gate[...] = (hidden_grad * rise[core]).astype(BF16)
        to_up[...] = (hidden_grad * swish[core]).astype(BF16)
        grads[:, 2 * core * units : (2 * core + 1) * units] = to_gate[...]
        grads[:, (2 * core + 1) * units : 2 * (core + 1) * units] = to_up[...]

    columns = slice(None)
    put_sums(jnp.dot(grads[...], across[:, columns], preferred_element_type=F32), columns, *sends)


def weight_grads_body(*refs):
    blocks = refs[:8]
    gate_grad, up_grad, hidden = [(refs[8 + i], refs[11].at[i]) for i in range(3)]
    into_gate, into_up, into_down = refs[12:]
    layer = jnp.concatenate([block[0] for block in blocks], 0)
    for grad, into in ((gate_grad, into_gate), (up_grad, into_up)):
        grad = jnp.concatenate([grad[0][...], grad[1][...]], 0)
        into[0] = contract_rows(layer, grad).astype(BF16)
    hidden = jnp.concatenate([hidden[0][...], hidden[1][...]], 0)
    cotangent = jnp.concatenate([block[1] for block in blocks], 0)
    into_down[0] = contract_rows(hidden, cotangent).astype(BF16)


def weight_grads(*args):
    _, rows, width = args[0].shape
    tokens, units = args[8].shape
    part = width // 4
    streamed = [pl.BlockSpec((2, rows, part), lambda i: (0, 0, i))] * 8
    whole = [pl.BlockSpec((tokens, units), lambda i: (0, 0))] * 3 + [pl.BlockSpec((3, tokens, units), lambda i: (0, 0, 0))]
    across = [pl.BlockSpec((1, part, units), lambda i: (0, i, 0))] * 2
    along = [pl.BlockSpec((1, units, part), lambda i: (0, 0, i))]
    shapes = [(1, width, units), (1, width, units), (1, units, width)]
    return pl.pallas_call(
        weight_grads_body,
        grid=(width // part,),
        out_shape=[jax.ShapeDtypeStruct(shape, BF16) for shape in shapes],
        in_specs=streamed + whole,
        out_specs=across + along,
        compiler_params=pltpu.CompilerParams(vmem_limit_bytes=24 * 2**20),
        cost_estimate=pl.CostEstimate(flops=0, bytes_accessed=0, transcendentals=0),
    )(*args)


def add_terms(terms, joined, at):
    own, *received = terms
    for half in (0, 1):
        rows = slice(16 * half, 16 * half + 16)
        sums = own[rows, :]
        for term in received:
            sums = sums + term[rows, :].astype(F32)
        for i in range(4):
            joined[(4 * half + i, *at)] = sums[4 * i : 4 * i + 4].astype(BF16)


def out_total_body(*refs):
    add_terms(refs[:4], refs[4], ())


def join_body(out_total, *refs):
    joined = refs[4]
    for i in range(NZ):
        joined[i, 0] = out_total[i]
    add_terms(refs[:4], joined, (1,))


def copy_body(source, target):
    target[...] = source[...]


def send_sums(own, last, next_, step):
    return [own, y_last(last), y_next(next_), z_step(step)]


def on_device(activations, w_gate, w_up, w_down, out_grad):
    arrived = from_behind(activations[0], "section", 1)
    rows, width = arrived.shape
    units = w_down.shape[1]
    tokens = NY * NZ * rows
    (out_grad,) = local_kernel(copy_body, [(out_grad.shape, BF16)], out_grad)
    (mine,) = local_kernel(fan_body, [((NZ, 2, rows, width), BF16)], arrived, out_grad)
    got = colour_all_to_all(mine)

    got, *partner = lax.optimization_barrier((got, swap(w_gate), swap(w_up), swap(w_down)))

    (own,) = local_kernel(split_body, [((2, NZ * rows, width), BF16)], got)
    next_, last, step = y_next(own), y_last(own), z_step(own)
    loaded = load(after(w_gate, own), w_up, w_down)
    weights = [w for pair in zip(loaded, partner) for w in pair]
    turned = local_kernel(
        turn_body, [((4 * units, width), BF16), ((width, 2 * units), BF16)],
        loaded[0], loaded[1], partner[0], partner[1], loaded[2], partner[2])
    next_, last = lax.optimization_barrier((next_, last, *turned))[:2]
    blocks = [own, next_, last, step]

    send = ((NZ * rows, width), BF16)
    sends = [((NZ * rows, width), F32), send, send, send]
    some = ((tokens, units), BF16)
    scratch = [pltpu.VMEM((tokens, width), BF16)]
    kept = ((2, tokens, units), F32)
    hidden, hidden_other, swish, rise, *out_sums = local_kernel(
        forward_body, [some, some, kept, kept, *sends], *blocks, *weights, scratch=scratch)
    out_terms = send_sums(*out_sums)
    gate_grad, up_grad, give, *back_sums = local_kernel(
        backward_body, [some, some, ((3, tokens, units), BF16), *sends],
        *blocks, *turned, swish, rise, hidden_other,
        scratch=scratch + [pltpu.VMEM((tokens, 4 * units), BF16)])
    back_terms = send_sums(*back_sums)

    (out_total,) = local_kernel(out_total_body, [((NZ, rows, width), BF16)], *out_terms)
    (sums,) = local_kernel(join_body, [((NZ, 2, rows, width), BF16)], out_total, *back_terms)

    *blocks, give = lax.optimization_barrier((*blocks, give, sums))[:-1]
    grad_gate, grad_up, grad_down = weight_grads(
        *blocks, *[swap(block) for block in blocks], gate_grad, up_grad, hidden, swap(give))
    arrived = colour_all_to_all(sums)
    arrived, grad_gate, grad_up, grad_down = lax.optimization_barrier((arrived, grad_gate, grad_up, grad_down))
    total = ((1, rows, width), BF16)
    (back,) = local_kernel(functools.partial(total_body, 1), [total], arrived)
    returned = from_behind(back, "section", -1)
    (output,) = local_kernel(functools.partial(total_body, 0), [total], arrived)
    (returned,) = local_kernel(copy_body, [total], returned)
    return (output, returned, grad_gate, grad_up, grad_down)


def solution(mesh):
    return jax.shard_map(
        on_device,
        mesh=mesh,
        in_specs=(
            P("section", PLANE, None),
            P("section", None, PLANE),
            P("section", None, PLANE),
            P("section", PLANE, None),
            P("section", PLANE, None),
        ),
        out_specs=(
            P("section", PLANE, None),
            P("section", PLANE, None),
            P("section", None, PLANE),
            P("section", None, PLANE),
            P("section", PLANE, None),
        ),
        check_vma=False,
    )
```
